256 devices in a mesh: dp: 64 (over z, x, core), tensor: 4 (over y).
Axes of the slice: x: 4, y: 4, z: 8, core: 2. Of those that a mesh axis runs over, the one named last changes fastest.
Arguments:
- acts: bfloat16 [32768, 8192], P(('dp', 'tensor')), may hold values from -6 to 6
- key_grad: bfloat16 [32768, 1024], P('dp', 'tensor'), may hold values from -0.25 to 0.25
- w_key: bfloat16 [8192, 1024], P(None, 'tensor'), may hold values from -6 to 6
- error_fb: float32 [524288, 1024], P('dp', 'tensor'), may hold values from -6 to 6
- q_prev: float32 [1024, 64], P('tensor'), may hold values from -6 to 6
Outputs:
- act_grad: bfloat16 [32768, 8192], P(('dp', 'tensor'))
- update: bfloat16 [8192, 1024], P(None, 'tensor')
- q_new: float32 [1024, 64], P('tensor')
The draws below stay inside these ranges and needn't reach their ends.
All inputs are finite; a program needn't handle non-finite values.
Results may differ from the reference program's by a relative error of at most 0.015.
Values may be sent and summed in bfloat16 or wider, within the bound.
No kernel may reach another device: no remote copies, remote signals or barrier semaphores. Data moves between devices by JAX's collectives and lax.ppermute only.
A program may use at most 128 MiB of HBM per device.

```python
import jax
import jax.numpy as jnp
from jax import lax

D = 8192
KVH = 8
HD = 128
R = 64
ROWS = 128
TOKENS = 32768
KV = 1024
N_DP = 64
N_TENSOR = 4


def levels(rng, dims, pieces, least, high):
    gain = 1.0
    for dim, blocks in pieces:
        heights = jax.random.uniform(jax.random.fold_in(jax.random.fold_in(rng, 6), dim), (blocks,), jnp.float32, least / len(pieces), high / len(pieces))
        gain = gain * jnp.repeat(jnp.exp(heights), dims[dim] // blocks).reshape((-1,) + (1,) * (len(dims) - 1 - dim))
    return gain


def noise(own_key, dims, width, limit, split=(), kind=jnp.bfloat16):
    gain = levels(own_key, dims, split, -0.22, 0.18) if split else 1.0
    result = jax.random.normal(own_key, dims, jnp.float32) * width * gain
    return jnp.minimum(jnp.maximum(result, -limit), limit).astype(kind)


def setup_inputs(seed: int = 0) -> dict:
    keys = jax.random.split(jax.random.key(seed), 6)
    return {
        "acts": noise(keys[0], (TOKENS, D), 1.0, 6.0, ((0, 256),)),
        "key_grad": noise(keys[1], (TOKENS, KV), (ROWS * N_TENSOR) ** -0.5, 0.25, ((0, 64), (1, 4))),
        "w_key": noise(keys[2], (D, KV), 1.0, 6.0, ((1, 4),)),
        "error_fb": noise(keys[3], (N_DP * D, KV), 1.0, 6.0, ((0, 64), (1, 4)), jnp.float32),
        "q_prev": noise(keys[4], (KV, R), 1.0, 6.0, ((0, 4),), jnp.float32),
    }


def reference(acts, key_grad, w_key, error_fb, q_prev):
    group_rows = ROWS * N_TENSOR
    col_block = KVH * HD // N_TENSOR
    act_groups = acts.reshape(N_DP, group_rows, D)
    grad_groups = key_grad.reshape(N_DP, group_rows, KVH * HD)
    err_groups = error_fb.reshape(N_DP, D, KVH * HD)
    w_blocks = w_key.astype(jnp.float32).reshape(D, N_TENSOR, col_block)

    def one_group(p_total, group_items):
        act_part, grad_part, err_part = group_items
        weight_grad = jnp.dot(act_part.T.astype(jnp.float32), grad_part.astype(jnp.float32), preferred_element_type=jnp.float32)
        merged = weight_grad + err_part
        p_local = jnp.einsum('dc,cr->rd', merged, q_prev, precision=lax.Precision.HIGHEST)
        g_blocks = grad_part.astype(jnp.float32).reshape(group_rows, N_TENSOR, col_block)
        partials = jnp.einsum('gtc,dtc->tgd', g_blocks, w_blocks)
        rounded = lax.optimization_barrier(partials.astype(jnp.bfloat16)).astype(jnp.float32)
        act_out = jnp.sum(rounded, axis=0).astype(jnp.bfloat16)
        return (p_total + p_local, (act_out, merged))
    start_p = jnp.zeros((R, D), jnp.float32)
    p_total, (act_outs, merged_all) = lax.scan(one_group, start_p, (act_groups, grad_groups, err_groups))
    gram_mat = jnp.einsum('rd,sd->rs', p_total, p_total, precision=lax.Precision.HIGHEST)
    factor = jnp.linalg.cholesky(gram_mat)
    p_hat = lax.linalg.triangular_solve(factor, p_total, left_side=True, lower=True)
    q_new = jnp.einsum('ndc,rd->cr', merged_all, p_hat, precision=lax.Precision.HIGHEST)
    update = jnp.einsum('rd,cr->dc', p_hat, q_new, precision=lax.Precision.HIGHEST)
    return (act_outs.reshape(N_DP * group_rows, D), update.astype(jnp.bfloat16), q_new)
```

```python
import jax
import jax.numpy as jnp
from jax import lax
from jax.sharding import Mesh, PartitionSpec as P

F32 = jnp.float32
BF = jnp.bfloat16
N_Z, N_X, N_C, N_Y = 8, 4, 2, 4


def dot(a, b, ca, cb):
    return lax.dot_general(a, b, (((ca,), (cb,)), ((), ())), preferred_element_type=F32)


def shift(v, axis, n, k):
    return lax.ppermute(v, axis, [(i, (i + k) % n) for i in range(n)])


def pick(v, i):
    return lax.dynamic_index_in_dim(v, i, 0, keepdims=False)


def y_scatter_sum(blocks, me):
    total = pick(blocks, me).astype(F32)
    for k in range(1, N_Y):
        sent = shift(pick(blocks, (me + k) % N_Y).astype(BF), "y", N_Y, k)
        total = total + sent.astype(F32)
    return total


def sum_all(p):
    me = lax.axis_index("c")
    half = p.reshape(2, 128, 16, 128)
    got = shift(pick(half, 1 - me).astype(BF), "c", 2, 1)
    own = (pick(half, me) + got.astype(F32)).astype(BF)
    got = lax.all_to_all(own, ("x", "y"), 0, 0, tiled=True)
    own = got.reshape(16, 8, 16, 128).astype(F32).sum(0).astype(BF)
    got = lax.all_to_all(jnp.broadcast_to(own[None], (8, 8, 16, 128)), "z", 0, 0, tiled=True)
    own = got.astype(F32).sum(0).astype(BF)
    got = lax.all_to_all(jnp.broadcast_to(own[None], (16, 8, 16, 128)), ("x", "y"), 0, 0, tiled=True)
    own = got.reshape(128, 16, 128)
    other = shift(own, "c", 2, 1)
    first = jnp.where(me == 0, own, other)
    second = jnp.where(me == 0, other, own)
    return jnp.concatenate([first, second], 0)


def sum_dp(q):
    b = q.astype(BF)
    b = (b.astype(F32) + shift(b, "c", 2, 1).astype(F32)).astype(BF)
    v = [b.astype(F32)] + [shift(b, "x", N_X, k).astype(F32) for k in range(1, N_X)]
    b = ((v[0] + v[2]) + (v[1] + v[3])).astype(BF)
    b = jnp.broadcast_to(b[None], (8, 64, 256))
    return lax.all_to_all(b, "z", 0, 0, tiled=True).astype(F32).sum(0)


def local(acts, key_grad, w_key, error_fb, q_prev):
    y = lax.axis_index("y")
    q_bf = q_prev.astype(BF)
    kgq = dot(q_bf, key_grad, 0, 1)
    kgq = y_scatter_sum(kgq.reshape(64, 4, 128).transpose(1, 0, 2), y)
    act_grad = lax.psum_scatter(
        dot(key_grad, w_key, 1, 1).astype(BF), "y", scatter_dimension=0, tiled=True
    )
    err = error_fb.astype(BF)
    p = dot(q_bf, err, 0, 1) + dot(kgq.astype(BF), acts, 1, 0)
    p = p.reshape(4, 16, 64, 128).transpose(2, 0, 1, 3).reshape(256, 16, 128)
    p = sum_all(p)
    p = p.reshape(64, 4, 16, 128).transpose(1, 2, 0, 3).reshape(64, 8192)
    ap = dot(p, acts, 1, 1).astype(BF)
    ap = [ap] + [shift(ap, "y", N_Y, k) for k in range(1, N_Y)]
    q_err = dot(p, err, 1, 0)
    kg = key_grad.reshape(4, 128, 256)
    q = q_err
    for k in range(N_Y):
        q = q + dot(ap[k], pick(kg, (y - k) % N_Y), 1, 0)
    gram = dot(p, p, 1, 1)
    factor = jnp.linalg.cholesky(gram)
    inv = lax.linalg.triangular_solve(factor, jnp.eye(64, dtype=F32), left_side=True, lower=True)
    q = sum_dp(q)
    q_new = jnp.dot(inv, q, precision=lax.Precision.HIGHEST)
    mix = lax.dot_general(inv, q_new, (((0,), (0,)), ((), ())), precision=lax.Precision.HIGHEST)
    update = dot(p, mix.astype(BF), 0, 0).astype(BF)
    return act_grad, update, q_new.T


def solution(mesh):
    fine = Mesh(mesh.devices.reshape(N_Z, N_X, N_C, N_Y), ("z", "x", "c", "y"))
    dp = ("z", "x", "c")
    rows = P(dp + ("y",), None)
    placed = (rows, P(dp, "y"), P(None, "y"), P(dp, "y"), P("y", None))
    return jax.shard_map(
        local,
        mesh=fine,
        in_specs=placed,
        out_specs=(rows, P(None, "y"), P("y", None)),
        check_vma=False,
    )
```

```python
import functools

import jax
import jax.numpy as jnp
from jax import lax
from jax.experimental import pallas as pl
from jax.experimental.pallas import tpu as pltpu
from jax.sharding import Mesh, PartitionSpec as P

F32 = jnp.float32
BF = jnp.bfloat16
N_Z, N_X, N_C, N_Y = 8, 4, 2, 4
D, RANK, COLS, ROWS = 8192, 64, 256, 128
LANES = 128
CHUNKS = D // LANES
HALF = CHUNKS // 2
STEP = 8
SPAN = STEP * LANES
VMEM = 48 * 1024 * 1024


def dot(a, b, ca, cb):
    return lax.dot_general(a, b, (((ca,), (cb,)), ((), ())), preferred_element_type=F32)


def shift(v, axis, n, k):
    return lax.ppermute(v, axis, [(i, (i + k) % n) for i in range(n)])


def pick(v, i):
    return lax.dynamic_index_in_dim(v, i, 0, keepdims=False)


def call(body, name, grid, scalars, in_specs, out_specs, out_shape, scratch, flops, nbytes):
    return pl.pallas_call(
        body,
        name=name,
        grid_spec=pltpu.PrefetchScalarGridSpec(
            num_scalar_prefetch=scalars,
            grid=grid,
            in_specs=in_specs,
            out_specs=out_specs,
            scratch_shapes=scratch,
        ),
        out_shape=out_shape,
        compiler_params=pltpu.CompilerParams(vmem_limit_bytes=VMEM),
        cost_estimate=pl.CostEstimate(flops=flops, bytes_accessed=nbytes, transcendentals=0),
    )


def whole(shape):
    return pl.BlockSpec(shape, lambda i, *s: (0,) * len(shape))


def partial_body(kg, w, out):
    out[...] = dot(kg[...], w[...], 1, 1).astype(BF)


def partial_grad(kg, w):
    n = kg.shape[0]
    return call(
        partial_body, "partial", (D // SPAN,), 0,
        [whole((n, COLS)), pl.BlockSpec((SPAN, COLS), lambda i: (i, 0))],
        pl.BlockSpec((n, SPAN), lambda i: (0, i)),
        jax.ShapeDtypeStruct((n, D), BF), [], 2 * n * COLS * D, 2 * D * (COLS + n),
    )(kg, w)


def left_body(h, q, kgq, err, acts, out):
    p = dot(q[...], err[...].astype(BF), 1, 1) + dot(kgq[...], acts[...], 1, 0)
    for j in range(STEP):
        out[j] = p[:, j * LANES:(j + 1) * LANES].astype(out.dtype)


def left(half, q, kgq, err, acts):
    n = HALF // STEP
    return call(
        left_body, "left", (n,), 1,
        [
            whole((RANK, COLS)),
            whole((RANK, ROWS)),
            pl.BlockSpec((SPAN, COLS), lambda i, h: (h[0] * n + i, 0)),
            pl.BlockSpec((ROWS, SPAN), lambda i, h: (0, h[0] * n + i)),
        ],
        pl.BlockSpec((STEP, RANK, LANES), lambda i, h: (i, 0, 0)),
        jax.ShapeDtypeStruct((HALF, RANK, LANES), BF), [],
        D * RANK * (COLS + ROWS), D // 2 * (COLS * 4 + ROWS * 2 + RANK * 2),
    )(half, q, kgq, err, acts)


def row(p):
    return jnp.concatenate([p[j] for j in range(STEP)], axis=1)


def add_to(out, value):
    @pl.when(pl.program_id(0) == 0)
    def _():
        out[...] = value

    @pl.when(pl.program_id(0) > 0)
    def _():
        out[...] += value


def act_body(h, p, acts, out):
    add_to(out, dot(row(p), acts[...], 1, 1))


def err_body(h, p, err, q, gram):
    v = row(p)
    add_to(q, dot(v, err[...].astype(BF), 1, 0))
    add_to(gram, dot(v, v, 1, 1))


def act_side(half, p, acts):
    n = HALF // STEP
    return call(
        act_body, "acts_p", (n,), 1,
        [
            pl.BlockSpec((STEP, RANK, LANES), lambda i, h: (i, 0, 0)),
            pl.BlockSpec((ROWS, SPAN), lambda i, h: (0, h[0] * n + i)),
        ],
        whole((RANK, ROWS)),
        jax.ShapeDtypeStruct((RANK, ROWS), F32), [],
        D * RANK * ROWS, D * (ROWS + RANK),
    )(half, p, acts)


def err_side(half, p, err):
    n = HALF // STEP
    return call(
        err_body, "err_p", (n,), 1,
        [
            pl.BlockSpec((STEP, RANK, LANES), lambda i, h: (i, 0, 0)),
            pl.BlockSpec((SPAN, COLS), lambda i, h: (h[0] * n + i, 0)),
        ],
        [whole((RANK, COLS)), whole((RANK, RANK))],
        [jax.ShapeDtypeStruct((RANK, COLS), F32), jax.ShapeDtypeStruct((RANK, RANK), F32)], [],
        D * RANK * (COLS + RANK), D * (COLS * 2 + RANK),
    )(half, p, err)


def right_body(y, qa, qb, a0, a1, a2, a3, kg, out):
    q = qa[...] + qb[...]
    for k, a in enumerate((a0, a1, a2, a3)):
        start = pl.multiple_of(lax.rem(y[0] + N_Y - k, N_Y) * ROWS, ROWS)
        q = q + dot(a[...], kg[pl.ds(start, ROWS), :], 1, 0)
    out[...] = q


def right(y, qa, qb, ap, kg):
    return call(
        right_body, "right", (1,), 1,
        [whole((RANK, COLS))] * 2 + [whole((RANK, ROWS))] * 4 + [whole((N_Y * ROWS, COLS))],
        whole((RANK, COLS)),
        jax.ShapeDtypeStruct((RANK, COLS), F32), [],
        2 * RANK * COLS * ROWS * N_Y, 4 * 10**5,
    )(y, qa, qb, *ap, kg)


def update_body(c, own, other, mix, out):
    p = jnp.where(pl.program_id(0) < HALF // STEP, own[...], other[...])
    for j in range(STEP):
        two = jnp.concatenate([p[j], p[j]], axis=0)
        out[j * LANES:(j + 1) * LANES, :] = dot(two, mix[...], 0, 0).astype(BF)


def update_from(c, own, other, mix):
    n = HALF // STEP
    return call(
        update_body, "update", (2 * n,), 1,
        [
            pl.BlockSpec((STEP, RANK, LANES), lambda i, c: (jnp.minimum(i, n - 1), 0, 0)),
            pl.BlockSpec((STEP, RANK, LANES), lambda i, c: (jnp.maximum(i - n, 0), 0, 0)),
            whole((2 * RANK, COLS)),
        ],
        pl.BlockSpec((SPAN, COLS), lambda i, c: (lax.rem(i + c[0] * n, 2 * n), 0)),
        jax.ShapeDtypeStruct((D, COLS), BF), [],
        4 * D * RANK * COLS, 2 * D * (RANK + COLS),
    )(c, own, other, mix)


def pairs(v):
    return (v[0] + v[2]) + (v[1] + v[3])


def ring4(b, axis):
    v = [b.astype(F32)] + [shift(b, axis, 4, k).astype(F32) for k in (1, 2, 3)]
    return pairs(v)


def local(acts, key_grad, w_key, error_fb, q_prev):
    y, c = lax.axis_index("y"), lax.axis_index("c")
    y1, c1 = y.astype(jnp.int32)[None], c.astype(jnp.int32)[None]
    q_t = q_prev.T.astype(BF)
    kgq = dot(q_t, key_grad, 1, 1)
    kgq = kgq.reshape(RANK, N_Y, ROWS).transpose(1, 0, 2)
    kgq, kg = lax.optimization_barrier((kgq, key_grad))
    sent = [shift(pick(kgq, (y + k) % N_Y).astype(BF), "y", N_Y, k) for k in (1, 2, 3)]

    act_grad = lax.psum_scatter(partial_grad(kg, w_key), "y", scatter_dimension=0, tiled=True)

    kgq = pick(kgq, y) + sum(s.astype(F32) for s in sent)
    kgq = kgq.astype(BF)
    give = left(1 - c1, q_t, kgq, error_fb, acts)
    got = shift(give, "c", 2, 1)
    p = left(c1, q_t, kgq, error_fb, acts)
    p = (p.astype(F32) + got.astype(F32)).astype(BF)
    p = lax.all_to_all(p, ("z", "x"), 0, 0, tiled=True).astype(F32).sum(0).astype(BF)
    p = ring4(p, "y").astype(BF)
    p = jnp.broadcast_to(p[None], (HALF, RANK, LANES))
    own = lax.all_to_all(p, ("z", "x"), 0, 0, tiled=True)

    other = shift(own, "c", 2, 1)
    ap_own = act_side(c1, own, acts)
    qa, gram_a = err_side(c1, own, error_fb)
    ap = (ap_own + act_side(1 - c1, other, acts)).astype(BF)
    ap = [ap] + [shift(ap, "y", N_Y, k) for k in (1, 2, 3)]
    qb, gram_b = err_side(1 - c1, other, error_fb)
    gram = gram_a + gram_b
    q = right(y1, qa, qb, ap, key_grad)

    q = q + shift(q, "c", 2, 1)
    q = ring4(q, "x").astype(BF)
    q, gram = lax.optimization_barrier((q, gram))
    q = lax.all_to_all(jnp.broadcast_to(q[None], (N_Z, RANK, COLS)), "z", 0, 0, tiled=True)
    factor = jnp.linalg.cholesky(gram)
    inv = lax.linalg.triangular_solve(factor, jnp.eye(RANK, dtype=F32), left_side=True, lower=True)
    q = q.astype(F32).sum(0)
    q_new = jnp.dot(inv, q, precision=lax.Precision.HIGHEST)
    mix = lax.dot_general(inv, q_new, (((0,), (0,)), ((), ())), precision=lax.Precision.HIGHEST)
    high = mix.astype(BF)
    low = (mix - high.astype(F32)).astype(BF)
    update = update_from(c1, own, other, jnp.concatenate([high, low], 0))
    return act_grad, update, q_new.T


def solution(mesh):
    fine = Mesh(mesh.devices.reshape(N_Z, N_X, N_C, N_Y), ("z", "x", "c", "y"))
    dp = ("z", "x", "c")
    rows = P(dp + ("y",), None)
    return jax.shard_map(
        local,
        mesh=fine,
        in_specs=(rows, P(dp, "y"), P(None, "y"), P(dp, "y"), P("y", None)),
        out_specs=(rows, P(None, "y"), P("y", None)),
        check_vma=False,
    )
```

```python
import jax
import jax.numpy as jnp
from jax import lax
from jax.experimental import pallas as pl
from jax.experimental.pallas import tpu as pltpu
from jax.sharding import Mesh, PartitionSpec as P

F32 = jnp.float32
BF = jnp.bfloat16
N_Z, N_X, N_C, N_Y = 8, 4, 2, 4
D, RANK, COLS, ROWS = 8192, 64, 256, 128
LANES = 128
CHUNKS = D // LANES
HALF = CHUNKS // 2
STEP = 8
SPAN = STEP * LANES
STEPS = HALF // STEP
PARTS = 4
IN_VMEM = pl.BlockSpec(memory_space=pltpu.VMEM)
IN_SMEM = pl.BlockSpec(memory_space=pltpu.SMEM)
IN_HBM = pl.BlockSpec(memory_space=pltpu.HBM)


def dot(a, b, ca, cb):
    return lax.dot_general(a, b, (((ca,), (cb,)), ((), ())), preferred_element_type=F32)


def shift(v, axis, n, k):
    return lax.ppermute(v, axis, [(i, (i + k) % n) for i in range(n)])


def kernel(body, name, ins, outs, out_shape, flops, nbytes, scratch=(), mib=8):
    return pl.pallas_call(
        body,
        name=name,
        in_specs=ins,
        out_specs=outs,
        out_shape=out_shape,
        scratch_shapes=list(scratch),
        compiler_params=pltpu.CompilerParams(vmem_limit_bytes=mib * 1024 * 1024),
        cost_estimate=pl.CostEstimate(flops=flops, bytes_accessed=nbytes, transcendentals=0),
    )


def shape(s, dtype):
    return jax.ShapeDtypeStruct(s, dtype)


def at(half, i):
    return pl.multiple_of(half * (D // 2) + i * SPAN, SPAN)


def tie(first, then):
    return lax.optimization_barrier((first, then))


def small_body(y, q, kg, q_t, own, s1, s2, s3):
    qt = q[...].T.astype(BF)
    q_t[...] = qt
    for k, out in enumerate((own, s1, s2, s3)):
        start = pl.multiple_of(lax.rem(y[0] + k, N_Y) * ROWS, ROWS)
        out[...] = dot(qt, kg[pl.ds(start, ROWS), :], 1, 1).astype(out.dtype)


def small(y, q, kg):
    block = (RANK, ROWS)
    return kernel(
        small_body, "small", [IN_SMEM, IN_VMEM, IN_VMEM], [IN_VMEM] * 5,
        [shape((RANK, COLS), BF), shape(block, F32)] + [shape(block, BF)] * 3,
        2 * RANK * COLS * ROWS * N_Y, 4 * 10**5,
    )(y, q, kg)


def partial_body(kg, w, out, kg_in, w_in, held, sem_kg, sem_w, sem_out):
    n = D // PARTS

    def load(i):
        span = pl.ds(i * n, n)
        return pltpu.make_async_copy(w.at[span], w_in.at[span], sem_w.at[i])

    def store(i):
        cols = pl.ds(i * n, n)
        return pltpu.make_async_copy(held.at[:, cols], out.at[:, cols], sem_out.at[i])

    first = pltpu.make_async_copy(kg, kg_in, sem_kg)
    first.start()
    for i in range(PARTS):
        load(i).start()
    first.wait()
    for i in range(PARTS):
        load(i).wait()
        for j in range(n // SPAN):
            cols = slice(i * n + j * SPAN, i * n + (j + 1) * SPAN)
            held[:, cols] = dot(kg_in[...], w_in[cols, :], 1, 1).astype(BF)
        store(i).start()
    for i in range(PARTS):
        store(i).wait()


def partial_grad(kg, w):
    n = kg.shape[0]
    dma = pltpu.SemaphoreType.DMA
    return kernel(
        partial_body, "partial", [IN_HBM, IN_HBM], IN_HBM, pltpu.HBM((n, D), BF),
        2 * n * COLS * D, 2 * D * (COLS + n),
        [
            pltpu.VMEM((n, COLS), BF), pltpu.VMEM((D, COLS), BF), pltpu.VMEM((n, D), BF),
            dma(()), dma((PARTS,)), dma((PARTS,)),
        ],
        24,
    )(*(pltpu.with_memory_space_constraint(v, pltpu.HBM) for v in (kg, w)))


def error_body(q, err, pe, eb, held, sem):
    def load(i):
        span = pl.ds(i * SPAN, SPAN)
        return pltpu.make_async_copy(err.at[span], held.at[span], sem.at[i])

    for i in range(D // SPAN):
        load(i).start()
    for i in range(D // SPAN):
        load(i).wait()
        span = slice(i * SPAN, (i + 1) * SPAN)
        e = held[span, :].astype(BF)
        eb[span, :] = e
        p = dot(q[...], e, 1, 1)
        for j in range(STEP):
            pe[i * STEP + j] = p[:, j * LANES:(j + 1) * LANES]


def error_side(q, err):
    return kernel(
        error_body, "error", [IN_VMEM, IN_HBM], [IN_VMEM, IN_VMEM],
        [pltpu.VMEM((CHUNKS, RANK, LANES), F32), pltpu.VMEM((D, COLS), BF)],
        2 * D * RANK * COLS, D * (COLS * 6 + RANK * 4),
        [pltpu.VMEM((D, COLS), F32), pltpu.SemaphoreType.DMA((D // SPAN,))], 16,
    )(q, pltpu.with_memory_space_constraint(err, pltpu.HBM))


def left_body(h, k0, k1, k2, k3, pe, acts, out):
    kgq = k0[...]
    for k in (k1, k2, k3):
        kgq = kgq + k[...].astype(F32)
    kgq = kgq.astype(BF)
    for i in range(STEPS):
        p = dot(kgq, acts[:, pl.ds(at(h[0], i), SPAN)], 1, 0)
        for j in range(STEP):
            k = i * STEP + j
            out[k] = (p[:, j * LANES:(j + 1) * LANES] + pe[h[0] * HALF + k]).astype(out.dtype)


def left(half, kgq, pe, acts, dtype):
    return kernel(
        left_body, "left", [IN_SMEM] + [IN_VMEM] * 6, IN_VMEM,
        shape((HALF, RANK, LANES), dtype),
        D * RANK * ROWS, D // 2 * (ROWS * 2 + RANK * 6),
    )(half, *kgq, pe, acts)


def rows(p, i):
    return jnp.concatenate([p[i * STEP + j] for j in range(STEP)], axis=1)


def act_body(h, p, acts, out):
    out[...] = sum(dot(rows(p, i), acts[:, pl.ds(at(h[0], i), SPAN)], 1, 1) for i in range(STEPS))


def act_side(half, p, acts):
    return kernel(
        act_body, "acts_p", [IN_SMEM, IN_VMEM, IN_VMEM], IN_VMEM, shape((RANK, ROWS), F32),
        D * RANK * ROWS, D * (ROWS + RANK),
    )(half, p, acts)


def err_body(h, p, err, out):
    out[...] = sum(
        dot(rows(p, i), err[pl.ds(at(h[0], i), SPAN), :], 1, 0) for i in range(STEPS)
    )


def err_side(half, p, err):
    return kernel(
        err_body, "err_p", [IN_SMEM, IN_VMEM, IN_VMEM], IN_VMEM, shape((RANK, COLS), F32),
        D * RANK * COLS, D * (COLS * 2 + RANK),
    )(half, p, err)


def right_body(y, qa, qb, a0, a1, a2, a3, kg, out):
    q = qa[...] + qb[...]
    for k, a in enumerate((a0, a1, a2, a3)):
        start = pl.multiple_of(lax.rem(y[0] + N_Y - k, N_Y) * ROWS, ROWS)
        q = q + dot(a[...], kg[pl.ds(start, ROWS), :], 1, 0)
    out[...] = q


def right(y, qa, qb, ap, kg):
    return kernel(
        right_body, "right", [IN_SMEM] + [IN_VMEM] * 7, IN_VMEM, shape((RANK, COLS), F32),
        2 * RANK * COLS * ROWS * N_Y, 4 * 10**5,
    )(y, qa, qb, *ap, kg)


def inverse_body(own, other, out):
    gram = jnp.zeros((RANK, RANK), F32)
    for p in (own, other):
        for i in range(STEPS):
            v = rows(p, i)
            gram = gram + dot(v, v, 1, 1)
    r = lax.broadcasted_iota(jnp.int32, (RANK, RANK), 0)
    c = lax.broadcasted_iota(jnp.int32, (RANK, RANK), 1)
    m = jnp.concatenate([gram, jnp.where(r == c, 1.0, 0.0)], axis=1)
    line = lax.broadcasted_iota(jnp.int32, (RANK, 1), 0)
    scale = jnp.zeros((RANK, 1), F32)
    for k in range(RANK):
        pivot = m[k:k + 1, k:k + 1]
        scale = jnp.where(line == k, lax.rsqrt(pivot), scale)
        if k < RANK - 1:
            f = jnp.where(line > k, m[:, k:k + 1] / pivot, 0.0)
            m = m - f * m[k:k + 1, :]
    out[...] = m[:, RANK:] * scale


def inverse(own, other):
    return kernel(
        inverse_body, "inverse", [IN_VMEM, IN_VMEM], IN_VMEM, shape((RANK, RANK), F32),
        2 * D * RANK * RANK, 4 * D * RANK,
    )(own, other)


def update_body(c, own, other, mix, out, held, sem):
    def copy(half):
        span = pl.ds(pl.multiple_of(half * (D // 2), D // 2), D // 2)
        return pltpu.make_async_copy(held.at[span], out.at[span], sem.at[half])

    for half, p in ((c[0], own), (1 - c[0], other)):
        for i in range(STEPS):
            v = rows(p, i)
            v = jnp.concatenate([v, v], axis=0)
            held[pl.ds(at(half, i), SPAN), :] = dot(v, mix[...], 0, 0).astype(BF)
        copy(half).start()
    copy(c[0]).wait()
    copy(1 - c[0]).wait()


def update_from(c, own, other, mix):
    return kernel(
        update_body, "update", [IN_SMEM] + [IN_VMEM] * 3, IN_HBM, shape((D, COLS), BF),
        4 * D * RANK * COLS, 2 * D * (RANK + COLS),
        [pltpu.VMEM((D, COLS), BF), pltpu.SemaphoreType.DMA((2,))], 12,
    )(c, own, other, mix)


def merge_body(v, out):
    total = v[0].astype(F32)
    for i in range(1, v.shape[0]):
        total = total + v[i].astype(F32)
    total = total.astype(BF)
    for i in range(out.shape[0]):
        out[i] = total


def merge(v, copies):
    block = v.shape[1:]
    size = v.size // v.shape[0]
    return kernel(
        merge_body, "merge", [IN_VMEM], IN_VMEM, shape((copies,) + block, BF),
        v.size, 2 * size * (v.shape[0] + copies),
    )(v)


def pairs_body(a, b, c, d, out):
    total = ((a[...] + c[...]) + (b[...] + d[...])).astype(BF)
    for i in range(out.shape[0]):
        out[i] = total


def ring_sum(v, axis, copies):
    v = [v] + [shift(v, axis, 4, k) for k in (1, 2, 3)]
    return kernel(
        pairs_body, "pairs", [IN_VMEM] * 4, IN_VMEM, shape((copies,) + v[0].shape, BF),
        4 * v[0].size, 2 * v[0].size * (8 + copies),
    )(*v)


def exchange(v, axes):
    return lax.all_to_all(v, axes, 0, 0, tiled=True)


def sum_left(p):
    n = HALF // 16
    p = merge(exchange(p, ("x", "y")).reshape(16, n, RANK, LANES), N_Z)
    p = merge(exchange(p, "z"), 16)
    return exchange(p, ("x", "y")).reshape(HALF, RANK, LANES)


def local(acts, key_grad, w_key, error_fb, q_prev):
    y = lax.axis_index("y").astype(jnp.int32)[None]
    c = lax.axis_index("c").astype(jnp.int32)[None]
    part = partial_grad(key_grad, w_key)
    act_grad = lax.psum_scatter(part, "y", scatter_dimension=0, tiled=True)
    q_t, k0, k1, k2, k3 = small(y, q_prev, key_grad)
    k1, q_t = tie(k1, q_t)
    kgq = [k0] + [shift(v, "y", N_Y, k) for k, v in ((1, k1), (2, k2), (3, k3))]
    pe, err = error_side(q_t, error_fb)

    got = shift(left(1 - c, kgq, pe, acts, BF), "c", 2, 1)
    p = left(c, kgq, pe, acts, F32)
    own = sum_left((p + got.astype(F32)).astype(BF))

    other = shift(own, "c", 2, 1)
    ap = act_side(c, own, acts)
    qa = err_side(c, own, err)
    ap = (ap + act_side(1 - c, other, acts)).astype(BF)
    ap = [ap] + [shift(ap, "y", N_Y, k) for k in (1, 2, 3)]
    qb = err_side(1 - c, other, err)
    q = right(y, qa, qb, ap, key_grad)

    q = q + shift(q, "c", 2, 1)
    q = ring_sum(q, "x", N_Z)
    q, other = tie(q, other)
    q = exchange(q, "z")
    inv = inverse(own, other)
    q = q.astype(F32).sum(0)
    q_new = jnp.dot(inv, q, precision=lax.Precision.HIGHEST)
    mix = lax.dot_general(inv, q_new, (((0,), (0,)), ((), ())), precision=lax.Precision.HIGHEST)
    high = mix.astype(BF)
    low = (mix - high.astype(F32)).astype(BF)
    update = update_from(c, own, other, jnp.concatenate([high, low], 0))
    return act_grad, update, q_new.T


def solution(mesh):
    fine = Mesh(mesh.devices.reshape(N_Z, N_X, N_C, N_Y), ("z", "x", "c", "y"))
    dp = ("z", "x", "c")
    rows_of = P(dp + ("y",), None)
    return jax.shard_map(
        local,
        mesh=fine,
        in_specs=(rows_of, P(dp, "y"), P(None, "y"), P(dp, "y"), P("y", None)),
        out_specs=(rows_of, P(None, "y"), P("y", None)),
        check_vma=False,
    )
```

```python
import jax
import jax.numpy as jnp
from jax import lax
from jax.experimental import pallas as pl
from jax.experimental.pallas import tpu as pltpu
from jax.sharding import Mesh, PartitionSpec as P

F32 = jnp.float32
BF = jnp.bfloat16
N_Z, N_X, N_C, N_Y = 8, 4, 2, 4
D, RANK, COLS, ROWS = 8192, 64, 256, 128
LANES = 128
CHUNKS = D // LANES
HALF = CHUNKS // 2
STEP = 8
SPAN = STEP * LANES
STEPS = HALF // STEP
PARTS = 4
IN_VMEM = pl.BlockSpec(memory_space=pltpu.VMEM)
IN_SMEM = pl.BlockSpec(memory_space=pltpu.SMEM)
IN_HBM = pl.BlockSpec(memory_space=pltpu.HBM)


def dot(a, b, ca, cb):
    return lax.dot_general(a, b, (((ca,), (cb,)), ((), ())), preferred_element_type=F32)


def shift(v, axis, n, k):
    return lax.ppermute(v, axis, [(i, (i + k) % n) for i in range(n)])


def kernel(body, name, ins, outs, out_shape, flops, nbytes, scratch=(), mib=8):
    return pl.pallas_call(
        body,
        name=name,
        in_specs=ins,
        out_specs=outs,
        out_shape=out_shape,
        scratch_shapes=list(scratch),
        compiler_params=pltpu.CompilerParams(vmem_limit_bytes=mib * 1024 * 1024),
        cost_estimate=pl.CostEstimate(flops=flops, bytes_accessed=nbytes, transcendentals=0),
    )


def shape(s, dtype):
    return jax.ShapeDtypeStruct(s, dtype)


def at(half, i):
    return pl.multiple_of(half * (D // 2) + i * SPAN, SPAN)


def tie(first, then):
    return lax.optimization_barrier((first, then))


def partial_body(y, q, kg, w, out, q_t, own, s1, s2, s3, kg_in, w_in, q_in, held, sem_in, sem_w, sem_out):
    n = D // PARTS

    def load(i):
        span = pl.ds(i * n, n)
        return pltpu.make_async_copy(w.at[span], w_in.at[span], sem_w.at[i])

    def store(i):
        cols = pl.ds(i * n, n)
        return pltpu.make_async_copy(held.at[:, cols], out.at[:, cols], sem_out.at[i])

    kg_copy = pltpu.make_async_copy(kg, kg_in, sem_in.at[0])
    q_copy = pltpu.make_async_copy(q, q_in, sem_in.at[1])
    kg_copy.start()
    for i in range(PARTS):
        load(i).start()
    q_copy.start()
    kg_copy.wait()
    for i in range(PARTS):
        load(i).wait()
        cols = slice(i * n, (i + 1) * n)
        held[:, cols] = dot(kg_in[...], w_in[cols, :], 1, 1).astype(BF)
        store(i).start()
    q_copy.wait()
    qt = q_in[...].astype(BF)
    q_t[...] = qt
    for k, block in enumerate((own, s1, s2, s3)):
        start = pl.multiple_of(lax.rem(y[0] + k, N_Y) * ROWS, ROWS)
        block[...] = dot(qt, kg_in[pl.ds(start, ROWS), :], 1, 1).astype(block.dtype)
    for i in range(PARTS):
        store(i).wait()


def partial_grad(y, q, kg, w):
    n = kg.shape[0]
    dma = pltpu.SemaphoreType.DMA
    block = (RANK, ROWS)
    return kernel(
        partial_body, "partial", [IN_SMEM] + [IN_HBM] * 3, [IN_HBM] + [IN_VMEM] * 5,
        [pltpu.HBM((n, D), BF), pltpu.VMEM((RANK, COLS), BF), pltpu.VMEM(block, F32)]
        + [pltpu.VMEM(block, BF)] * 3,
        2 * n * COLS * D, 2 * D * (COLS + n),
        [
            pltpu.VMEM((n, COLS), BF), pltpu.VMEM((D, COLS), BF), pltpu.VMEM((RANK, COLS), F32),
            pltpu.VMEM((n, D), BF), dma((2,)), dma((PARTS,)), dma((PARTS,)),
        ],
        24,
    )(y, *(pltpu.with_memory_space_constraint(v, pltpu.HBM) for v in (q, kg, w)))


def error_body(q, err, pe, eb, held, sem):
    def load(i):
        span = pl.ds(i * SPAN, SPAN)
        return pltpu.make_async_copy(err.at[span], held.at[span], sem.at[i])

    for i in range(D // SPAN):
        load(i).start()
    for i in range(D // SPAN):
        load(i).wait()
        span = slice(i * SPAN, (i + 1) * SPAN)
        e = held[span, :].astype(BF)
        eb[span, :] = e
        p = dot(q[...], e, 1, 1)
        for j in range(STEP):
            pe[i * STEP + j] = p[:, j * LANES:(j + 1) * LANES]


def error_side(q, err):
    return kernel(
        error_body, "error", [IN_VMEM, IN_HBM], [IN_VMEM, IN_VMEM],
        [pltpu.VMEM((CHUNKS, RANK, LANES), F32), pltpu.VMEM((D, COLS), BF)],
        2 * D * RANK * COLS, D * (COLS * 6 + RANK * 4),
        [pltpu.VMEM((D, COLS), F32), pltpu.SemaphoreType.DMA((D // SPAN,))], 16,
    )(q, pltpu.with_memory_space_constraint(err, pltpu.HBM))


def left_body(h, k0, k1, k2, k3, pe, acts, out):
    kgq = k0[...]
    for k in (k1, k2, k3):
        kgq = kgq + k[...].astype(F32)
    kgq = kgq.astype(BF)
    for i in range(STEPS):
        p = dot(kgq, acts[:, pl.ds(at(h[0], i), SPAN)], 1, 0)
        for j in range(STEP):
            k = i * STEP + j
            out[k] = (p[:, j * LANES:(j + 1) * LANES] + pe[h[0] * HALF + k]).astype(out.dtype)


def left(half, kgq, pe, acts, dtype):
    return kernel(
        left_body, "left", [IN_SMEM] + [IN_VMEM] * 6, IN_VMEM,
        shape((HALF, RANK, LANES), dtype),
        D * RANK * ROWS, D // 2 * (ROWS * 2 + RANK * 6),
    )(half, *kgq, pe, acts)


def rows(p, i):
    return jnp.concatenate([p[i * STEP + j] for j in range(STEP)], axis=1)


def act_body(h, p, acts, out):
    out[...] = sum(dot(rows(p, i), acts[:, pl.ds(at(h[0], i), SPAN)], 1, 1) for i in range(STEPS))


def act_side(half, p, acts):
    return kernel(
        act_body, "acts_p", [IN_SMEM, IN_VMEM, IN_VMEM], IN_VMEM, shape((RANK, ROWS), F32),
        D * RANK * ROWS, D * (ROWS + RANK),
    )(half, p, acts)


def err_body(h, p, err, out):
    out[...] = sum(
        dot(rows(p, i), err[pl.ds(at(h[0], i), SPAN), :], 1, 0) for i in range(STEPS)
    )


def err_side(half, p, err):
    return kernel(
        err_body, "err_p", [IN_SMEM, IN_VMEM, IN_VMEM], IN_VMEM, shape((RANK, COLS), F32),
        D * RANK * COLS, D * (COLS * 2 + RANK),
    )(half, p, err)


def right_body(y, qa, qb, a0, a1, a2, a3, kg, out):
    q = qa[...] + qb[...]
    for k, a in enumerate((a0, a1, a2, a3)):
        start = pl.multiple_of(lax.rem(y[0] + N_Y - k, N_Y) * ROWS, ROWS)
        q = q + dot(a[...], kg[pl.ds(start, ROWS), :], 1, 0)
    out[...] = q


def right(y, qa, qb, ap, kg):
    return kernel(
        right_body, "right", [IN_SMEM] + [IN_VMEM] * 7, IN_VMEM, shape((RANK, COLS), F32),
        2 * RANK * COLS * ROWS * N_Y, 4 * 10**5,
    )(y, qa, qb, *ap, kg)


def inverse_body(own, other, out):
    gram = jnp.zeros((RANK, RANK), F32)
    for p in (own, other):
        for i in range(STEPS):
            v = rows(p, i)
            gram = gram + dot(v, v, 1, 1)
    r = lax.broadcasted_iota(jnp.int32, (RANK, RANK), 0)
    c = lax.broadcasted_iota(jnp.int32, (RANK, RANK), 1)
    m = jnp.concatenate([gram, jnp.where(r == c, 1.0, 0.0)], axis=1)
    line = lax.broadcasted_iota(jnp.int32, (RANK, 1), 0)
    scale = jnp.zeros((RANK, 1), F32)
    for k in range(RANK):
        pivot = m[k:k + 1, k:k + 1]
        scale = jnp.where(line == k, lax.rsqrt(pivot), scale)
        if k < RANK - 1:
            f = jnp.where(line > k, m[:, k:k + 1] / pivot, 0.0)
            m = m - f * m[k:k + 1, :]
    out[...] = m[:, RANK:] * scale


def inverse(own, other):
    return kernel(
        inverse_body, "inverse", [IN_VMEM, IN_VMEM], IN_VMEM, shape((RANK, RANK), F32),
        2 * D * RANK * RANK, 4 * D * RANK,
    )(own, other)


def update_body(c, own, other, mix, out, held, sem):
    def copy(half, i):
        span = pl.ds(at(half, i), SPAN)
        return pltpu.make_async_copy(held.at[span], out.at[span], sem.at[half * STEPS + i])

    for half, p in ((c[0], own), (1 - c[0], other)):
        for i in range(STEPS):
            v = rows(p, i)
            v = jnp.concatenate([v, v], axis=0)
            held[pl.ds(at(half, i), SPAN), :] = dot(v, mix[...], 0, 0).astype(BF)
            copy(half, i).start()
    for half in (c[0], 1 - c[0]):
        for i in range(STEPS):
            copy(half, i).wait()


def update_from(c, own, other, mix):
    return kernel(
        update_body, "update", [IN_SMEM] + [IN_VMEM] * 3, IN_HBM, pltpu.HBM((D, COLS), BF),
        4 * D * RANK * COLS, 2 * D * (RANK + COLS),
        [pltpu.VMEM((D, COLS), BF), pltpu.SemaphoreType.DMA((2 * STEPS,))], 12,
    )(c, own, other, mix)


def merge_body(v, out):
    total = v[0].astype(F32)
    for i in range(1, v.shape[0]):
        total = total + v[i].astype(F32)
    total = total.astype(BF)
    for i in range(out.shape[0]):
        out[i] = total


def merge(v, copies):
    block = v.shape[1:]
    size = v.size // v.shape[0]
    return kernel(
        merge_body, "merge", [IN_VMEM], IN_VMEM, shape((copies,) + block, BF),
        v.size, 2 * size * (v.shape[0] + copies),
    )(v)


def pairs_body(a, b, c, d, out):
    a, b, c, d = (v[...].astype(F32) for v in (a, b, c, d))
    total = ((a + c) + (b + d)).astype(BF)
    for i in range(out.shape[0]):
        out[i] = total


def ring_sum(v, axis, copies):
    v = [v] + [shift(v, axis, 4, k) for k in (1, 2, 3)]
    return kernel(
        pairs_body, "pairs", [IN_VMEM] * 4, IN_VMEM, shape((copies,) + v[0].shape, BF),
        4 * v[0].size, 2 * v[0].size * (4 + copies),
    )(*v)


def exchange(v, axes):
    return lax.all_to_all(v, axes, 0, 0, tiled=True)


def sum_left(p):
    n = HALF // 16
    p = merge(exchange(p, ("x", "y")).reshape(16, n, RANK, LANES), N_Z)
    p = merge(exchange(p, "z"), 16)
    return exchange(p, ("x", "y")).reshape(HALF, RANK, LANES)


def local(acts, key_grad, w_key, error_fb, q_prev):
    y = lax.axis_index("y").astype(jnp.int32)[None]
    c = lax.axis_index("c").astype(jnp.int32)[None]
    part, q_t, k0, k1, k2, k3 = partial_grad(y, q_prev.T, key_grad, w_key)
    act_grad = lax.psum_scatter(part, "y", scatter_dimension=0, tiled=True)
    kgq = [k0] + [shift(v, "y", N_Y, k) for k, v in ((1, k1), (2, k2), (3, k3))]
    pe, err = error_side(q_t, error_fb)

    got = shift(left(1 - c, kgq, pe, acts, BF), "c", 2, 1)
    p = left(c, kgq, pe, acts, F32)
    own = sum_left((p + got.astype(F32)).astype(BF))

    other = shift(own, "c", 2, 1)
    ap = act_side(c, own, acts)
    qa = err_side(c, own, err)
    ap = (ap + act_side(1 - c, other, acts)).astype(BF)
    ap = [ap] + [shift(ap, "y", N_Y, k) for k in (1, 2, 3)]
    qb = err_side(1 - c, other, err)
    q = right(y, qa, qb, ap, key_grad)

    q = (q + shift(q, "c", 2, 1)).astype(BF)
    q = ring_sum(q, "x", N_Z)
    q, other = tie(q, other)
    q = exchange(q, "z")
    inv = inverse(own, other)
    q = q.astype(F32).sum(0)
    q_new = jnp.dot(inv, q, precision=lax.Precision.HIGHEST)
    mix = lax.dot_general(inv, q_new, (((0,), (0,)), ((), ())), precision=lax.Precision.HIGHEST)
    high = mix.astype(BF)
    low = (mix - high.astype(F32)).astype(BF)
    update = update_from(c, own, other, jnp.concatenate([high, low], 0))
    return act_grad, update, q_new.T


def solution(mesh):
    fine = Mesh(mesh.devices.reshape(N_Z, N_X, N_C, N_Y), ("z", "x", "c", "y"))
    dp = ("z", "x", "c")
    rows_of = P(dp + ("y",), None)
    return jax.shard_map(
        local,
        mesh=fine,
        in_specs=(rows_of, P(dp, "y"), P(None, "y"), P(dp, "y"), P("y", None)),
        out_specs=(rows_of, P(None, "y"), P("y", None)),
        check_vma=False,
    )
```

```python
import jax
import jax.numpy as jnp
from jax import lax
from jax.experimental import pallas as pl
from jax.experimental.pallas import tpu as pltpu
from jax.sharding import Mesh, PartitionSpec as P

F32 = jnp.float32
BF = jnp.bfloat16
N_Z, N_X, N_C, N_Y = 8, 4, 2, 4
PAIR = 2
D, RANK, COLS, ROWS = 8192, 64, 256, 128
LANES = 128
CHUNKS = D // LANES
HALF = CHUNKS // 2
STEP = 8
SPAN = STEP * LANES
STEPS = HALF // STEP
PARTS = 4
IN_VMEM = pl.BlockSpec(memory_space=pltpu.VMEM)
IN_SMEM = pl.BlockSpec(memory_space=pltpu.SMEM)
IN_HBM = pl.BlockSpec(memory_space=pltpu.HBM)


def dot(a, b, ca, cb):
    return lax.dot_general(a, b, (((ca,), (cb,)), ((), ())), preferred_element_type=F32)


def shift(v, axis, n, k):
    return lax.ppermute(v, axis, [(i, (i + k) % n) for i in range(n)])


def kernel(body, name, ins, outs, out_shape, flops, nbytes, scratch=(), mib=8):
    return pl.pallas_call(
        body,
        name=name,
        in_specs=ins,
        out_specs=outs,
        out_shape=out_shape,
        scratch_shapes=list(scratch),
        compiler_params=pltpu.CompilerParams(vmem_limit_bytes=mib * 1024 * 1024),
        cost_estimate=pl.CostEstimate(flops=flops, bytes_accessed=nbytes, transcendentals=0),
    )


def shape(s, dtype):
    return jax.ShapeDtypeStruct(s, dtype)


def at(half, i):
    return pl.multiple_of(half * (D // 2) + i * SPAN, SPAN)


def tie(first, then):
    return lax.optimization_barrier((first, then))


def partial_body(y, q, kg, w, out, q_t, own, s1, s2, s3, kg_in, w_in, q_in, held, sem_in, sem_w, sem_out):
    n = D // PARTS

    def load(i):
        span = pl.ds(i * n, n)
        return pltpu.make_async_copy(w.at[span], w_in.at[span], sem_w.at[i])

    def store(i):
        cols = pl.ds(i * n, n)
        return pltpu.make_async_copy(held.at[:, cols], out.at[:, cols], sem_out.at[i])

    kg_copy = pltpu.make_async_copy(kg, kg_in, sem_in.at[0])
    q_copy = pltpu.make_async_copy(q, q_in, sem_in.at[1])
    kg_copy.start()
    for i in range(PARTS):
        load(i).start()
    q_copy.start()
    kg_copy.wait()
    for i in range(PARTS):
        load(i).wait()
        cols = slice(i * n, (i + 1) * n)
        held[:, cols] = dot(kg_in[...], w_in[cols, :], 1, 1).astype(BF)
        store(i).start()
    q_copy.wait()
    qt = q_in[...].astype(BF)
    q_t[...] = qt
    for k, block in enumerate((own, s1, s2, s3)):
        start = pl.multiple_of(lax.rem(y[0] + k, N_Y) * ROWS, ROWS)
        block[...] = dot(qt, kg_in[pl.ds(start, ROWS), :], 1, 1).astype(block.dtype)
    for i in range(PARTS):
        store(i).wait()


def partial_grad(y, q, kg, w):
    n = kg.shape[0]
    dma = pltpu.SemaphoreType.DMA
    block = (RANK, ROWS)
    return kernel(
        partial_body, "partial", [IN_SMEM] + [IN_HBM] * 3, [IN_HBM] + [IN_VMEM] * 5,
        [pltpu.HBM((n, D), BF), pltpu.VMEM((RANK, COLS), BF), pltpu.VMEM(block, F32)]
        + [pltpu.VMEM(block, BF)] * 3,
        2 * n * COLS * D, 2 * D * (COLS + n),
        [
            pltpu.VMEM((n, COLS), BF), pltpu.VMEM((D, COLS), BF), pltpu.VMEM((RANK, COLS), F32),
            pltpu.VMEM((n, D), BF), dma((2,)), dma((PARTS,)), dma((PARTS,)),
        ],
        24,
    )(y, *(pltpu.with_memory_space_constraint(v, pltpu.HBM) for v in (q, kg, w)))


def error_body(q, err, pe, eb, held, sem):
    def load(i):
        span = pl.ds(i * SPAN, SPAN)
        return pltpu.make_async_copy(err.at[span], held.at[span], sem.at[i])

    for i in range(D // SPAN):
        load(i).start()
    for i in range(D // SPAN):
        load(i).wait()
        span = slice(i * SPAN, (i + 1) * SPAN)
        e = held[span, :].astype(BF)
        eb[span, :] = e
        p = dot(q[...], e, 1, 1)
        for j in range(STEP):
            pe[i * STEP + j] = p[:, j * LANES:(j + 1) * LANES]


def error_side(q, err):
    return kernel(
        error_body, "error", [IN_VMEM, IN_HBM], [IN_VMEM, IN_VMEM],
        [pltpu.VMEM((CHUNKS, RANK, LANES), F32), pltpu.VMEM((D, COLS), BF)],
        2 * D * RANK * COLS, D * (COLS * 6 + RANK * 4),
        [pltpu.VMEM((D, COLS), F32), pltpu.SemaphoreType.DMA((D // SPAN,))], 16,
    )(q, pltpu.with_memory_space_constraint(err, pltpu.HBM))


def left_body(h, k0, k1, k2, k3, pe, acts, out):
    kgq = k0[...]
    for k in (k1, k2, k3):
        kgq = kgq + k[...].astype(F32)
    kgq = kgq.astype(BF)
    for i in range(STEPS):
        p = dot(kgq, acts[:, pl.ds(at(h[0], i), SPAN)], 1, 0)
        for j in range(STEP):
            k = i * STEP + j
            out[k] = (p[:, j * LANES:(j + 1) * LANES] + pe[h[0] * HALF + k]).astype(out.dtype)


def left(half, kgq, pe, acts, dtype):
    return kernel(
        left_body, "left", [IN_SMEM] + [IN_VMEM] * 6, IN_VMEM,
        shape((HALF, RANK, LANES), dtype),
        D * RANK * ROWS, D // 2 * (ROWS * 2 + RANK * 6),
    )(half, *kgq, pe, acts)


def rows(p, i):
    return jnp.concatenate([p[i * STEP + j] for j in range(STEP)], axis=1)


def act_body(h, p, acts, out):
    out[...] = sum(dot(rows(p, i), acts[:, pl.ds(at(h[0], i), SPAN)], 1, 1) for i in range(STEPS))


def act_side(half, p, acts):
    return kernel(
        act_body, "acts_p", [IN_SMEM, IN_VMEM, IN_VMEM], IN_VMEM, shape((RANK, ROWS), F32),
        D * RANK * ROWS, D * (ROWS + RANK),
    )(half, p, acts)


def err_body(h, p, err, out):
    out[...] = sum(
        dot(rows(p, i), err[pl.ds(at(h[0], i), SPAN), :], 1, 0) for i in range(STEPS)
    )


def err_side(half, p, err):
    return kernel(
        err_body, "err_p", [IN_SMEM, IN_VMEM, IN_VMEM], IN_VMEM, shape((RANK, COLS), F32),
        D * RANK * COLS, D * (COLS * 2 + RANK),
    )(half, p, err)


def right_body(y, qa, qb, a0, a1, a2, a3, kg, out):
    q = qa[...] + qb[...]
    for k, a in enumerate((a0, a1, a2, a3)):
        start = pl.multiple_of(lax.rem(y[0] + N_Y - k, N_Y) * ROWS, ROWS)
        q = q + dot(a[...], kg[pl.ds(start, ROWS), :], 1, 0)
    out[...] = q


def right(y, qa, qb, ap, kg):
    return kernel(
        right_body, "right", [IN_SMEM] + [IN_VMEM] * 7, IN_VMEM, shape((RANK, COLS), F32),
        2 * RANK * COLS * ROWS * N_Y, 4 * 10**5,
    )(y, qa, qb, *ap, kg)


def inverse_body(own, other, out):
    gram = jnp.zeros((RANK, RANK), F32)
    for p in (own, other):
        for i in range(STEPS):
            v = rows(p, i)
            gram = gram + dot(v, v, 1, 1)
    r = lax.broadcasted_iota(jnp.int32, (RANK, RANK), 0)
    c = lax.broadcasted_iota(jnp.int32, (RANK, RANK), 1)
    m = jnp.concatenate([gram, jnp.where(r == c, 1.0, 0.0)], axis=1)
    line = lax.broadcasted_iota(jnp.int32, (RANK, 1), 0)
    scale = jnp.zeros((RANK, 1), F32)
    for k in range(RANK):
        pivot = m[k:k + 1, k:k + 1]
        scale = jnp.where(line == k, lax.rsqrt(pivot), scale)
        if k < RANK - 1:
            f = jnp.where(line > k, m[:, k:k + 1] / pivot, 0.0)
            m = m - f * m[k:k + 1, :]
    out[...] = m[:, RANK:] * scale


def inverse(own, other):
    return kernel(
        inverse_body, "inverse", [IN_VMEM, IN_VMEM], IN_VMEM, shape((RANK, RANK), F32),
        2 * D * RANK * RANK, 4 * D * RANK,
    )(own, other)


def update_body(c, own, other, mix, out, held, sem):
    def copy(half, i):
        span = pl.ds(at(half, i), SPAN)
        return pltpu.make_async_copy(held.at[span], out.at[span], sem.at[half * STEPS + i])

    for half, p in ((c[0], own), (1 - c[0], other)):
        for i in range(STEPS):
            v = rows(p, i)
            v = jnp.concatenate([v, v], axis=0)
            held[pl.ds(at(half, i), SPAN), :] = dot(v, mix[...], 0, 0).astype(BF)
            copy(half, i).start()
    for half in (c[0], 1 - c[0]):
        for i in range(STEPS):
            copy(half, i).wait()


def update_from(c, own, other, mix):
    return kernel(
        update_body, "update", [IN_SMEM] + [IN_VMEM] * 3, IN_HBM, pltpu.HBM((D, COLS), BF),
        4 * D * RANK * COLS, 2 * D * (RANK + COLS),
        [pltpu.VMEM((D, COLS), BF), pltpu.SemaphoreType.DMA((2 * STEPS,))], 12,
    )(c, own, other, mix)


def merge_body(v, out):
    total = v[0].astype(F32)
    for i in range(1, v.shape[0]):
        total = total + v[i].astype(F32)
    total = total.astype(BF)
    for i in range(out.shape[0]):
        out[i] = total


def merge(v, copies):
    block = v.shape[1:]
    size = v.size // v.shape[0]
    return kernel(
        merge_body, "merge", [IN_VMEM], IN_VMEM, shape((copies,) + block, BF),
        v.size, 2 * size * (v.shape[0] + copies),
    )(v)


def pairs_body(a, b, c, d, out):
    a, b, c, d = (v[...].astype(F32) for v in (a, b, c, d))
    total = ((a + c) + (b + d)).astype(BF)
    for i in range(out.shape[0]):
        out[i] = total


def ring_sum(v, axis, copies):
    v = [v] + [shift(v, axis, 4, k) for k in (1, 2, 3)]
    return kernel(
        pairs_body, "pairs", [IN_VMEM] * 4, IN_VMEM, shape((copies,) + v[0].shape, BF),
        4 * v[0].size, 2 * v[0].size * (4 + copies),
    )(*v)


def exchange(v, axes):
    return lax.all_to_all(v, axes, 0, 0, tiled=True)


def sum_left(p):
    axes = ("x", "zp", "y")
    p = merge(exchange(p, axes), N_Z // PAIR)
    p = merge(exchange(p, "zq"), HALF)
    return exchange(p, axes)


def local(acts, key_grad, w_key, error_fb, q_prev):
    y = lax.axis_index("y").astype(jnp.int32)[None]
    c = lax.axis_index("c").astype(jnp.int32)[None]
    part, q_t, k0, k1, k2, k3 = partial_grad(y, q_prev.T, key_grad, w_key)
    act_grad = lax.psum_scatter(part, "y", scatter_dimension=0, tiled=True)
    kgq = [k0] + [shift(v, "y", N_Y, k) for k, v in ((1, k1), (2, k2), (3, k3))]
    pe, err = error_side(q_t, error_fb)

    got = shift(left(1 - c, kgq, pe, acts, BF), "c", 2, 1)
    p = left(c, kgq, pe, acts, F32)
    own = sum_left((p + got.astype(F32)).astype(BF))

    other = shift(own, "c", 2, 1)
    ap = act_side(c, own, acts)
    qa = err_side(c, own, err)
    ap = (ap + act_side(1 - c, other, acts)).astype(BF)
    ap = [ap] + [shift(ap, "y", N_Y, k) for k in (1, 2, 3)]
    qb = err_side(1 - c, other, err)
    q = right(y, qa, qb, ap, key_grad)

    q = (q + shift(q, "c", 2, 1)).astype(BF)
    q = ring_sum(q, "x", N_Z)
    q, other = tie(q, other)
    q = exchange(q, ("zq", "zp"))
    inv = inverse(own, other)
    q = q.astype(F32).sum(0)
    q_new = jnp.dot(inv, q, precision=lax.Precision.HIGHEST)
    mix = lax.dot_general(inv, q_new, (((0,), (0,)), ((), ())), precision=lax.Precision.HIGHEST)
    high = mix.astype(BF)
    low = (mix - high.astype(F32)).astype(BF)
    update = update_from(c, own, other, jnp.concatenate([high, low], 0))
    return act_grad, update, q_new.T


def solution(mesh):
    dp = ("zq", "zp", "x", "c")
    fine = Mesh(mesh.devices.reshape(N_Z // PAIR, PAIR, N_X, N_C, N_Y), dp + ("y",))
    rows_of = P(dp + ("y",), None)
    return jax.shard_map(
        local,
        mesh=fine,
        in_specs=(rows_of, P(dp, "y"), P(None, "y"), P(dp, "y"), P("y", None)),
        out_specs=(rows_of, P(None, "y"), P("y", None)),
        check_vma=False,
    )
```

```python
import jax
import jax.numpy as jnp
from jax import lax
from jax.experimental import pallas as pl
from jax.experimental.pallas import tpu as pltpu
from jax.sharding import Mesh, PartitionSpec as P

F32 = jnp.float32
BF = jnp.bfloat16
N_Z, N_X, N_C, N_Y = 8, 4, 2, 4
PAIR = 2
D, RANK, COLS, ROWS = 8192, 64, 256, 128
LANES = 128
CHUNKS = D // LANES
HALF = CHUNKS // 2
STEP = 8
SPAN = STEP * LANES
STEPS = HALF // STEP
PARTS = 4
IN_VMEM = pl.BlockSpec(memory_space=pltpu.VMEM)
IN_SMEM = pl.BlockSpec(memory_space=pltpu.SMEM)
IN_HBM = pl.BlockSpec(memory_space=pltpu.HBM)


def dot(a, b, ca, cb):
    return lax.dot_general(a, b, (((ca,), (cb,)), ((), ())), preferred_element_type=F32)


def shift(v, axis, n, k):
    return lax.ppermute(v, axis, [(i, (i + k) % n) for i in range(n)])


def kernel(body, name, ins, outs, out_shape, flops, nbytes, scratch=(), mib=8):
    return pl.pallas_call(
        body,
        name=name,
        in_specs=ins,
        out_specs=outs,
        out_shape=out_shape,
        scratch_shapes=list(scratch),
        compiler_params=pltpu.CompilerParams(vmem_limit_bytes=mib * 1024 * 1024),
        cost_estimate=pl.CostEstimate(flops=flops, bytes_accessed=nbytes, transcendentals=0),
    )


def fold(v):
    return v[:RANK] + v[RANK:]


def shape(s, dtype):
    return jax.ShapeDtypeStruct(s, dtype)


def at(half, i):
    return pl.multiple_of(half * (D // 2) + i * SPAN, SPAN)


def tie(first, then):
    return lax.optimization_barrier((first, then))


def partial_body(y, q, kg, w, out, q_t, own, s1, s2, s3, kg_in, w_in, q_in, held, sem_in, sem_w, sem_out):
    n = D // PARTS

    def load(i):
        span = pl.ds(i * n, n)
        return pltpu.make_async_copy(w.at[span], w_in.at[span], sem_w.at[i])

    def store(i):
        cols = pl.ds(i * n, n)
        return pltpu.make_async_copy(held.at[:, cols], out.at[:, cols], sem_out.at[i])

    kg_copy = pltpu.make_async_copy(kg, kg_in, sem_in.at[0])
    q_copy = pltpu.make_async_copy(q, q_in, sem_in.at[1])
    kg_copy.start()
    for i in range(PARTS):
        load(i).start()
    q_copy.start()
    kg_copy.wait()
    for i in range(PARTS):
        load(i).wait()
        cols = slice(i * n, (i + 1) * n)
        held[:, cols] = dot(kg_in[...], w_in[cols, :], 1, 1).astype(BF)
        store(i).start()
    q_copy.wait()
    high = q_in[...].astype(BF)
    low = (q_in[...] - high.astype(F32)).astype(BF)
    qt = jnp.concatenate([high, low], axis=0)
    q_t[...] = qt
    for k, block in enumerate((own, s1, s2, s3)):
        start = pl.multiple_of(lax.rem(y[0] + k, N_Y) * ROWS, ROWS)
        block[...] = fold(dot(qt, kg_in[pl.ds(start, ROWS), :], 1, 1)).astype(block.dtype)
    for i in range(PARTS):
        store(i).wait()


def partial_grad(y, q, kg, w):
    n = kg.shape[0]
    dma = pltpu.SemaphoreType.DMA
    block = (RANK, ROWS)
    return kernel(
        partial_body, "partial", [IN_SMEM] + [IN_HBM] * 3, [IN_HBM] + [IN_VMEM] * 5,
        [pltpu.HBM((n, D), BF), pltpu.VMEM((2 * RANK, COLS), BF), pltpu.VMEM(block, F32)]
        + [pltpu.VMEM(block, BF)] * 3,
        2 * n * COLS * D, 2 * D * (COLS + n),
        [
            pltpu.VMEM((n, COLS), BF), pltpu.VMEM((D, COLS), BF), pltpu.VMEM((RANK, COLS), F32),
            pltpu.VMEM((n, D), BF), dma((2,)), dma((PARTS,)), dma((PARTS,)),
        ],
        24,
    )(y, *(pltpu.with_memory_space_constraint(v, pltpu.HBM) for v in (q, kg, w)))


def error_body(q, err, pe, eb, held, sem):
    def load(i):
        span = pl.ds(i * SPAN, SPAN)
        return pltpu.make_async_copy(err.at[span], held.at[span], sem.at[i])

    for i in range(D // SPAN):
        load(i).start()
    for i in range(D // SPAN):
        load(i).wait()
        span = slice(i * SPAN, (i + 1) * SPAN)
        e = held[span, :].astype(BF)
        eb[span, :] = e
        p = fold(dot(q[...], e, 1, 1))
        for j in range(STEP):
            pe[i * STEP + j] = p[:, j * LANES:(j + 1) * LANES]


def error_side(q, err):
    return kernel(
        error_body, "error", [IN_VMEM, IN_HBM], [IN_VMEM, IN_VMEM],
        [pltpu.VMEM((CHUNKS, RANK, LANES), F32), pltpu.VMEM((D, COLS), BF)],
        2 * D * RANK * COLS, D * (COLS * 6 + RANK * 4),
        [pltpu.VMEM((D, COLS), F32), pltpu.SemaphoreType.DMA((D // SPAN,))], 16,
    )(q, pltpu.with_memory_space_constraint(err, pltpu.HBM))


def left_body(h, k0, k1, k2, k3, pe, acts, out):
    kgq = k0[...]
    for k in (k1, k2, k3):
        kgq = kgq + k[...].astype(F32)
    kgq = kgq.astype(BF)
    for i in range(STEPS):
        p = dot(kgq, acts[:, pl.ds(at(h[0], i), SPAN)], 1, 0)
        for j in range(STEP):
            k = i * STEP + j
            out[k] = (p[:, j * LANES:(j + 1) * LANES] + pe[h[0] * HALF + k]).astype(out.dtype)


def left(half, kgq, pe, acts, dtype):
    return kernel(
        left_body, "left", [IN_SMEM] + [IN_VMEM] * 6, IN_VMEM,
        shape((HALF, RANK, LANES), dtype),
        D * RANK * ROWS, D // 2 * (ROWS * 2 + RANK * 6),
    )(half, *kgq, pe, acts)


def rows(p, i):
    return jnp.concatenate([p[i * STEP + j] for j in range(STEP)], axis=1)


def act_body(h, p, acts, out):
    out[...] = sum(dot(rows(p, i), acts[:, pl.ds(at(h[0], i), SPAN)], 1, 1) for i in range(STEPS))


def act_side(half, p, acts):
    return kernel(
        act_body, "acts_p", [IN_SMEM, IN_VMEM, IN_VMEM], IN_VMEM, shape((RANK, ROWS), F32),
        D * RANK * ROWS, D * (ROWS + RANK),
    )(half, p, acts)


def err_body(h, p, err, out):
    out[...] = sum(
        dot(rows(p, i), err[pl.ds(at(h[0], i), SPAN), :], 1, 0) for i in range(STEPS)
    )


def err_side(half, p, err):
    return kernel(
        err_body, "err_p", [IN_SMEM, IN_VMEM, IN_VMEM], IN_VMEM, shape((RANK, COLS), F32),
        D * RANK * COLS, D * (COLS * 2 + RANK),
    )(half, p, err)


def right_body(y, qa, qb, a0, a1, a2, a3, kg, out):
    q = qa[...] + qb[...]
    for k, a in enumerate((a0, a1, a2, a3)):
        start = pl.multiple_of(lax.rem(y[0] + N_Y - k, N_Y) * ROWS, ROWS)
        q = q + dot(a[...], kg[pl.ds(start, ROWS), :], 1, 0)
    out[...] = q


def right(y, qa, qb, ap, kg):
    return kernel(
        right_body, "right", [IN_SMEM] + [IN_VMEM] * 7, IN_VMEM, shape((RANK, COLS), F32),
        2 * RANK * COLS * ROWS * N_Y, 4 * 10**5,
    )(y, qa, qb, *ap, kg)


def inverse_body(own, other, out):
    gram = jnp.zeros((RANK, RANK), F32)
    for p in (own, other):
        for i in range(STEPS):
            v = rows(p, i)
            gram = gram + dot(v, v, 1, 1)
    r = lax.broadcasted_iota(jnp.int32, (RANK, RANK), 0)
    c = lax.broadcasted_iota(jnp.int32, (RANK, RANK), 1)
    m = jnp.concatenate([gram, jnp.where(r == c, 1.0, 0.0)], axis=1)
    line = lax.broadcasted_iota(jnp.int32, (RANK, 1), 0)
    scale = jnp.zeros((RANK, 1), F32)
    for k in range(RANK):
        pivot = m[k:k + 1, k:k + 1]
        scale = jnp.where(line == k, lax.rsqrt(pivot), scale)
        if k < RANK - 1:
            f = jnp.where(line > k, m[:, k:k + 1] / pivot, 0.0)
            m = m - f * m[k:k + 1, :]
    out[...] = m[:, RANK:] * scale


def inverse(own, other):
    return kernel(
        inverse_body, "inverse", [IN_VMEM, IN_VMEM], IN_VMEM, shape((RANK, RANK), F32),
        2 * D * RANK * RANK, 4 * D * RANK,
    )(own, other)


def update_body(c, own, other, mix, out, held, sem):
    def copy(half, i):
        span = pl.ds(at(half, i), SPAN)
        return pltpu.make_async_copy(held.at[span], out.at[span], sem.at[half * STEPS + i])

    for half, p in ((c[0], own), (1 - c[0], other)):
        for i in range(STEPS):
            v = rows(p, i)
            v = jnp.concatenate([v, v], axis=0)
            held[pl.ds(at(half, i), SPAN), :] = dot(v, mix[...], 0, 0).astype(BF)
            copy(half, i).start()
    for half in (c[0], 1 - c[0]):
        for i in range(STEPS):
            copy(half, i).wait()


def update_from(c, own, other, mix):
    return kernel(
        update_body, "update", [IN_SMEM] + [IN_VMEM] * 3, IN_HBM, pltpu.HBM((D, COLS), BF),
        4 * D * RANK * COLS, 2 * D * (RANK + COLS),
        [pltpu.VMEM((D, COLS), BF), pltpu.SemaphoreType.DMA((2 * STEPS,))], 12,
    )(c, own, other, mix)


def merge_body(v, out):
    total = v[0].astype(F32)
    for i in range(1, v.shape[0]):
        total = total + v[i].astype(F32)
    total = total.astype(BF)
    for i in range(out.shape[0]):
        out[i] = total


def merge(v, copies):
    block = v.shape[1:]
    size = v.size // v.shape[0]
    return kernel(
        merge_body, "merge", [IN_VMEM], IN_VMEM, shape((copies,) + block, BF),
        v.size, 2 * size * (v.shape[0] + copies),
    )(v)


def pairs_body(a, b, c, d, out):
    a, b, c, d = (v[...].astype(F32) for v in (a, b, c, d))
    total = ((a + c) + (b + d)).astype(BF)
    for i in range(out.shape[0]):
        out[i] = total


def ring_sum(v, axis, copies):
    v = [v] + [shift(v, axis, 4, k) for k in (1, 2, 3)]
    return kernel(
        pairs_body, "pairs", [IN_VMEM] * 4, IN_VMEM, shape((copies,) + v[0].shape, BF),
        4 * v[0].size, 2 * v[0].size * (4 + copies),
    )(*v)


def exchange(v, axes):
    return lax.all_to_all(v, axes, 0, 0, tiled=True)


def sum_left(p):
    axes = ("x", "zp", "y")
    p = merge(exchange(p, axes), N_Z // PAIR)
    p = merge(exchange(p, "zq"), HALF)
    return exchange(p, axes)


def local(acts, key_grad, w_key, error_fb, q_prev):
    y = lax.axis_index("y").astype(jnp.int32)[None]
    c = lax.axis_index("c").astype(jnp.int32)[None]
    part, q_t, k0, k1, k2, k3 = partial_grad(y, q_prev.T, key_grad, w_key)
    act_grad = lax.psum_scatter(part, "y", scatter_dimension=0, tiled=True)
    kgq = [k0] + [shift(v, "y", N_Y, k) for k, v in ((1, k1), (2, k2), (3, k3))]
    pe, err = error_side(q_t, error_fb)

    got = shift(left(1 - c, kgq, pe, acts, BF), "c", 2, 1)
    p = left(c, kgq, pe, acts, F32)
    own = sum_left((p + got.astype(F32)).astype(BF))

    other = shift(own, "c", 2, 1)
    ap = act_side(c, own, acts)
    qa = err_side(c, own, err)
    ap = (ap + act_side(1 - c, other, acts)).astype(BF)
    ap = [ap] + [shift(ap, "y", N_Y, k) for k in (1, 2, 3)]
    qb = err_side(1 - c, other, err)
    q = right(y, qa, qb, ap, key_grad)

    q = (q + shift(q, "c", 2, 1)).astype(BF)
    q = ring_sum(q, "x", N_Z)
    q, other = tie(q, other)
    q = exchange(q, ("zq", "zp"))
    inv = inverse(own, other)
    q = q.astype(F32).sum(0)
    q_new = jnp.dot(inv, q, precision=lax.Precision.HIGHEST)
    mix = lax.dot_general(inv, q_new, (((0,), (0,)), ((), ())), precision=lax.Precision.HIGHEST)
    high = mix.astype(BF)
    low = (mix - high.astype(F32)).astype(BF)
    update = update_from(c, own, other, jnp.concatenate([high, low], 0))
    return act_grad, update, q_new.T


def solution(mesh):
    dp = ("zq", "zp", "x", "c")
    fine = Mesh(mesh.devices.reshape(N_Z // PAIR, PAIR, N_X, N_C, N_Y), dp + ("y",))
    rows_of = P(dp + ("y",), None)
    return jax.shard_map(
        local,
        mesh=fine,
        in_specs=(rows_of, P(dp, "y"), P(None, "y"), P(dp, "y"), P("y", None)),
        out_specs=(rows_of, P(None, "y"), P("y", None)),
        check_vma=False,
    )
```
